256 devices in a mesh: row: 16 (over z, x_hi), col: 16 (over x_lo, y, core).
Axes of the slice: x: 4 (x_hi: 2, x_lo: 2; x = x_hi * 2 + x_lo), y: 4, z: 8, core: 2. Of those that a mesh axis runs over, the one named last changes fastest.
Arguments:
- records: float32 [65536, 128], P(('row', 'col')), may hold values from -6 to 6
- move_face: int32 [65536], P(('row', 'col')), may hold values from 0 to 4, as said below
- move_slot: int32 [65536], P(('row', 'col')), may hold values from 0 to 255
- pattern_s: int32 [1024, 20], P(('row', 'col')), may hold values from 0 to 1, as said below
- pattern_x: int32 [1024, 20], P(('row', 'col')), may hold values from 0 to 1, as said below
- start_inverse: float32 [65536, 1280], P(('row', 'col')), may hold values from -0.04 to 1.25
Outputs:
- migrated: float32 [65536, 128], P(('row', 'col'))
- inverse: float32 [65536, 1280], P(('row', 'col'))
The draws below stay inside these ranges and needn't reach their ends.
Inputs may be any that keep to these rules, and one draw needn't show every extreme that they name: `move_face`: on every device, among its 256 slots each of the faces 1, 2, 3, 4 is named at least once. `pattern_s`: symmetric as a relation between blocks; every block is coupled to itself. `pattern_x`: symmetric as a relation between blocks; ones wherever pattern_s has one.
All inputs are finite; a program needn't handle non-finite values.
Results may differ from the reference program's by a relative error of at most 0.0001.
Values sent between devices are 32-bit elements; how exact they have to be, the bound alone decides.
A program may use at most 64 MiB of HBM per device.

```python
import math
import jax
import jax.numpy as jnp
from jax import lax

BLK = 64
F = 128
BLK_DEV = 4
ITERS = 2
FUNC_DEV = 256
FUNCS = 65536
NB = 1024
N_ROW = 16
N_COL = 16


DIR_ROW = (0, -1, 1, 0, 0)


DIR_COL = (0, 0, 0, -1, 1)


def neighbour_table_drawn():
    devices = N_ROW * N_COL
    labels = jnp.arange(devices, dtype=jnp.int32)
    grid_row = labels // N_COL
    grid_col = labels % N_COL
    columns = [(grid_row + DIR_ROW[side]) % N_ROW * N_COL + (grid_col + DIR_COL[side]) % N_COL for side in range(5)]
    return jnp.stack(columns, axis=1).astype(jnp.int32)


def shared_bits(key):
    drawn = jax.random.randint(key, (NB, NB), 0, 1024)
    joint = drawn + drawn.T
    labels = jnp.arange(NB, dtype=jnp.int32)
    on_diagonal = labels[:, None] == labels[None, :]
    return jnp.where(on_diagonal | (joint < 1024), 1, 0).astype(jnp.int32)


def compact_pattern(bits):
    devices = N_ROW * N_COL
    neighbours = neighbour_table_drawn()
    local = jnp.arange(BLK_DEV, dtype=jnp.int32)
    row_ids = jnp.arange(devices, dtype=jnp.int32)[:, None, None, None] * BLK_DEV + local[None, :, None, None]
    col_ids = neighbours[:, None, :, None] * BLK_DEV + local[None, None, None, :]
    row_ids = jnp.broadcast_to(row_ids, (devices, BLK_DEV, 5, BLK_DEV))
    col_ids = jnp.broadcast_to(col_ids, (devices, BLK_DEV, 5, BLK_DEV))
    return bits[row_ids, col_ids].reshape(NB, 5 * BLK_DEV).astype(jnp.int32)


def draw_pattern_s(key, part):
    shared = shared_bits(key)
    return compact_pattern(shared)


def draw_pattern_x(key, part):
    shared = shared_bits(key)
    key = jax.random.fold_in(key, 7)
    further = shared_bits(key)
    return compact_pattern(jnp.maximum(shared, further))


def draw_move_face(key, part):
    key = jax.random.fold_in(key, 3)
    first_key, second_key = jax.random.split(key)
    devices = FUNCS // FUNC_DEV
    random_faces = jax.random.randint(first_key, (devices, FUNC_DEV), 0, 5)
    scores = jax.random.randint(second_key, (devices, FUNC_DEV), 0, 1 << 20) * FUNC_DEV + jnp.arange(FUNC_DEV, dtype=jnp.int32)[None, :]
    ranking = jnp.argsort(jnp.argsort(scores, axis=1), axis=1)
    faces = jnp.where(ranking < 4, ranking + 1, random_faces)
    return faces.reshape(-1).astype(jnp.int32)


def draw_start_inverse(key, part):
    key = jax.random.fold_in(key, 11)
    first_key, second_key = jax.random.split(key)
    noise_part = jnp.clip(jax.random.normal(first_key, (FUNCS, 5 * FUNC_DEV), jnp.float32) * 0.008, -0.04, 0.04)
    diagonal = jax.random.uniform(second_key, (FUNCS,), jnp.float32, 0.75, 1.25)
    row_ids = jnp.arange(FUNCS, dtype=jnp.int32) % FUNC_DEV
    col_ids = jnp.arange(5 * FUNC_DEV, dtype=jnp.int32)
    on_diagonal = row_ids[:, None] == col_ids[None, :]
    return jnp.where(on_diagonal, diagonal[:, None], noise_part).astype(jnp.float32)


def place_ends(values, key, low, top_value):
    spot = [jax.random.randint(jax.random.fold_in(key, axis), (), 0, length) for axis, length in enumerate(values.shape)]
    main_axis = values.shape.index(max(values.shape))
    beside = spot[:main_axis] + [(spot[main_axis] + 1) % values.shape[main_axis]] + spot[main_axis + 1:]
    return values.at[tuple(spot)].set(low).at[tuple(beside)].set(top_value)


def level_of(stream_key, shape, pieces, smallest, high):
    def one(dim, shards_of):
        draws = jax.random.uniform(jax.random.fold_in(jax.random.fold_in(stream_key, 6), dim), (shards_of,), jnp.float32, smallest / len(pieces), high / len(pieces))
        return jnp.repeat(jnp.exp(draws), shape[dim] // shards_of).reshape((-1,) + (1,) * (len(shape) - dim - 1))

    loudness = one(*pieces[0])
    for cut in pieces[1:]:
        loudness = loudness * one(*cut)
    return loudness


def normal_values(own_key, dims, scale, reach, cuts=(), kind=jnp.bfloat16):
    result = jax.random.normal(own_key, dims, jnp.float32) * scale
    if len(cuts) > 0:
        result = level_of(own_key, dims, cuts, -0.22, 0.18) * result
    return jnp.clip(result, min=-reach, max=reach).astype(kind)


def setup_inputs(seed: int = 0) -> dict:
    splits = jax.random.split(jax.random.key(seed), 7)
    return {
        "records": normal_values(splits[0], (FUNCS, F), 1.0, 6.0, ((0, 256),), jnp.float32),
        "move_face": draw_move_face(jax.random.fold_in(splits[6], 71), 0),
        "move_slot": place_ends(jax.random.randint(splits[2], (FUNCS,), 0, FUNC_DEV), jax.random.fold_in(splits[2], 1), 0, FUNC_DEV - 1).astype(jnp.int32),
        "pattern_s": draw_pattern_s(jax.random.fold_in(splits[6], 71), 0),
        "pattern_x": draw_pattern_x(jax.random.fold_in(splits[6], 71), 0),
        "start_inverse": draw_start_inverse(jax.random.fold_in(splits[6], 71), 0),
    }


COUPLE_BASE = 0.2
FULL = lax.Precision.HIGHEST
DIR_ROW = (0, -1, 1, 0, 0)
DIR_COL = (0, 0, 0, -1, 1)
TERMS = ((0, 0, 0), (0, 1, 1), (0, 2, 2), (0, 3, 3), (0, 4, 4), (1, 0, 2), (1, 1, 0), (2, 0, 1), (2, 2, 0), (3, 0, 4), (3, 3, 0), (4, 0, 3), (4, 4, 0))

def neighbour_table():
    devices = N_ROW * N_COL
    labels = jnp.arange(devices, dtype=jnp.int32)
    grid_row = labels // N_COL
    grid_col = labels % N_COL
    columns = [(grid_row + DIR_ROW[side]) % N_ROW * N_COL + (grid_col + DIR_COL[side]) % N_COL for side in range(5)]
    return jnp.stack(columns, axis=1).astype(jnp.int32)

def expand_blocks(pattern):
    block_rows, block_cols = pattern.shape
    flags = jnp.broadcast_to(pattern[:, None, :, None] > 0, (block_rows, BLK, block_cols, BLK))
    return flags.reshape(block_rows * BLK, block_cols * BLK)

def sparse_product(left, right, neighbours, retained):
    devices = neighbours.shape[0]
    left_groups = left.reshape(devices, FUNC_DEV, 5, FUNC_DEV)
    right_groups = right.reshape(devices, FUNC_DEV, 5, FUNC_DEV)
    outputs = []
    for target in range(5):
        summed = jnp.zeros((devices, FUNC_DEV, FUNC_DEV), jnp.float32)
        for source, aimed, taken in TERMS:
            if aimed == target:
                partner = right_groups[:, :, taken, :][neighbours[:, source]]
                summed = summed + jnp.einsum('dik,dkj->dij', left_groups[:, :, source, :], partner, precision=FULL, preferred_element_type=jnp.float32)
        outputs.append(summed)
    whole = jnp.stack(outputs, axis=2).reshape(devices * FUNC_DEV, 5 * FUNC_DEV)
    return jnp.where(retained, whole, 0.0)

def reference(records, move_face, move_slot, pattern_s, pattern_x, start_inverse):
    total_slots = records.shape[0]
    devices = N_ROW * N_COL
    slot_ids = jnp.arange(total_slots, dtype=jnp.int32)
    device = slot_ids // FUNC_DEV
    grid_row = device // N_COL
    grid_col = device % N_COL
    row_steps = jnp.array(DIR_ROW, dtype=jnp.int32)
    col_steps = jnp.array(DIR_COL, dtype=jnp.int32)
    source_row = (grid_row + row_steps[move_face]) % N_ROW
    source_col = (grid_col + col_steps[move_face]) % N_COL
    source = ((source_row * N_COL + source_col) * FUNC_DEV + move_slot).astype(jnp.int32)
    migrated = records[source]
    neighbours = neighbour_table()
    grouped = migrated.reshape(devices, FUNC_DEV, F)
    nearby = grouped[neighbours]
    gram_matrix = jnp.einsum('dif,dquf->diqu', grouped, nearby, precision=FULL, preferred_element_type=jnp.float32).reshape(total_slots, 5 * FUNC_DEV)
    coupling = COUPLE_BASE / math.sqrt(5 * F * FUNC_DEV)
    columns = jnp.arange(5 * FUNC_DEV, dtype=jnp.int32)
    identity_part = ((slot_ids % FUNC_DEV)[:, None] == columns[None, :]).astype(jnp.float32)
    correlation = jnp.where(expand_blocks(pattern_s), coupling * gram_matrix, 0.0) + identity_part
    retained = expand_blocks(pattern_x)
    inverse = jnp.where(retained, start_inverse, 0.0)
    for iteration in range(ITERS):
        product = sparse_product(correlation, inverse, neighbours, retained)
        correction = sparse_product(inverse, product, neighbours, retained)
        inverse = jnp.where(retained, 2.0 * inverse - correction, 0.0)
    return (migrated, inverse)
```

```python
import math

import jax
import jax.numpy as jnp
from jax import lax
from jax.experimental import pallas as pl
from jax.experimental.pallas import tpu as pltpu
from jax.sharding import PartitionSpec as P

BLK = 64
COUPLE_BASE = 0.2
F32 = jnp.float32
BF16 = jnp.bfloat16
MESH = pl.DeviceIdType.MESH

N = 256
FEAT = 128
CH = 4
CROWS = N // CH
WEST, EAST, NEAR, FAR = 0, 1, 2, 3
X0, P1, X1, P2 = 0, 1, 2, 3
RCH = 2
RROWS = N // RCH


def dot(a, b):
    return jnp.dot(a, b, preferred_element_type=F32)


def dot_nt(a, b):
    return lax.dot_general(a, b, (((1,), (1,)), ((), ())), preferred_element_type=F32)


def halves(x):
    high = x.astype(BF16)
    return high, (x - high.astype(F32)).astype(BF16)


def put_left(ref, x):
    high, low = halves(x)
    ref[:, 0:N] = high
    ref[:, N : 2 * N] = high
    ref[:, 2 * N : 3 * N] = low


def put_right(ref, x):
    high, low = halves(x)
    ref[0:N, :] = high
    ref[N : 2 * N, :] = low
    ref[2 * N : 3 * N, :] = high


def put_both(left, right, x):
    high, low = halves(x)
    left[:, 0:N] = high
    left[:, N : 2 * N] = high
    left[:, 2 * N : 3 * N] = low
    right[0:N, :] = high
    right[N : 2 * N, :] = low
    right[2 * N : 3 * N, :] = high


def make_kernel(n_row, n_col, coupling):
    def kernel(
        rec_hbm, face_ref, slot_ref, ps_ref, px_ref, x0_hbm,
        mig_out, inv_out,
        recs, pats, migs, opp, diag, own, xab, xba, outs,
        hot, split, mig_l, mig_r, rpat, sel, mask,
        eaa, eab, eba, ebb,
        xaa_l, x1aa_l, xab_l, xba_l, xbb_l,
        xaa_r, xab_r, xba_r, xbb_r, paa_r, pab_r, pba_r, pbb_r,
        loc, rec_s, rec_r, pat_s, pat_r, mig_s, mig_rs, opp_s, opp_r, dia_s, dia_r, out_s,
    ):
        r = lax.axis_index("row")
        c = lax.axis_index("col")
        odd = r % 2
        s = 1 - 2 * odd
        west = (r, (c + n_col - 1) % n_col)
        east = (r, (c + 1) % n_col)
        near = ((r + s + n_row) % n_row, c)
        far = ((r - s + n_row) % n_row, c)
        ahead = ((r + 2 * s + n_row) % n_row, c)
        behind = ((r - 2 * s + n_row) % n_row, c)
        group = (3, 4, 2 - odd, 1 + odd)
        direct = ((west, EAST), (east, WEST), (near, NEAR))

        def cols(q):
            return pl.ds(pl.multiple_of(q * N, N), N)

        local = []

        def fetch(src, dst):
            copy = pltpu.make_async_copy(src, dst, loc.at[len(local)])
            copy.start()
            local.append(copy)

        fetch(rec_hbm, recs.at[4])
        fetch(x0_hbm.at[:, 0:N], own.at[X0])
        for slot in range(4):
            fetch(x0_hbm.at[:, cols(group[slot])], xab.at[slot])

        pats[4] = jnp.zeros((8, 128), F32)
        pats[4, 0:4, 0:20] = jnp.where(ps_ref[...] > 0, 1.0, 0.0).astype(F32)
        pats[4, 4:8, 0:20] = jnp.where(px_ref[...] > 0, 1.0, 0.0).astype(F32)

        barrier = pltpu.get_barrier_semaphore()
        for other in (west, east, near, far, ahead, behind):
            pl.semaphore_signal(barrier, inc=1, device_id=other, device_id_type=MESH)
        pl.semaphore_wait(barrier, 6)

        sends = []

        def send(src, dst, ssem, rsem, device):
            copy = pltpu.make_async_remote_copy(
                src_ref=src, dst_ref=dst, send_sem=ssem, recv_sem=rsem, device_id=device, device_id_type=MESH
            )
            copy.start()
            sends.append(copy)

        def arrive(dst, ssem, rsem):
            pltpu.make_async_remote_copy(
                src_ref=dst, dst_ref=dst, send_sem=ssem, recv_sem=rsem, device_id=near, device_id_type=MESH
            ).wait_recv()

        def rrows(j):
            return pl.ds(j * RROWS, RROWS)

        def crows(j):
            return pl.ds(j * CROWS, CROWS)

        for j in range(RCH):
            for way in (2, 0, 1):
                device, theirs = direct[way]
                send(rec_hbm.at[rrows(j)], recs.at[theirs, rrows(j)], rec_s.at[way, j], rec_r.at[theirs, j], device)
        for way in (2, 0, 1):
            device, theirs = direct[way]
            send(pats.at[4], pats.at[theirs], pat_s.at[way], pat_r.at[theirs], device)
        for slot, (device, theirs) in ((FAR, (far, FAR)), (NEAR, (near, NEAR)), (WEST, direct[0]), (EAST, direct[1])):
            send(x0_hbm.at[:, cols(group[slot])], opp.at[theirs], opp_s.at[slot], opp_r.at[theirs], device)

        place = face_ref[...] * N + slot_ref[...]
        place = jnp.transpose(jnp.broadcast_to(place.astype(F32), (N, N)))
        lane = lax.broadcasted_iota(jnp.int32, (N, N), 1).astype(F32)
        for slot in range(5):
            q = 0 if slot == 4 else group[slot]
            first = (q * N * jnp.ones((1, 1), jnp.int32)).astype(F32)
            hot[:, slot * N : (slot + 1) * N] = jnp.where(place == lane + first, 1.0, 0.0).astype(BF16)

        row8 = lax.broadcasted_iota(jnp.int32, (N, 8), 0) // BLK
        col8 = lax.broadcasted_iota(jnp.int32, (N, 8), 1)
        spread_s = jnp.where(col8 == row8, 1.0, 0.0).astype(BF16)
        spread_x = jnp.where(col8 == row8 + 4, 1.0, 0.0).astype(BF16)
        row128 = lax.broadcasted_iota(jnp.int32, (N, 128), 0) // BLK
        col128 = lax.broadcasted_iota(jnp.int32, (N, 128), 1)
        for slot in range(5):
            q = 0 if slot == 4 else group[slot]
            sel[slot] = jnp.where(col128 == row128 + q * 4, 1.0, 0.0).astype(BF16)
        mine = pats[4].astype(BF16)
        rpat[0] = dot(spread_s, mine).astype(BF16)
        rpat[1] = dot(spread_x, mine).astype(BF16)

        for copy in local:
            copy.wait()

        def mask_slot(slot, carry):
            mask[slot] = dot_nt(rpat[1], sel[slot])
            mask[slot + 5] = dot_nt(sel[slot], rpat[1])
            block = xab[slot] * mask[slot]
            xab[slot] = block
            put_both(xab_l.at[slot], xab_r.at[slot], block)
            return carry

        mask[4] = dot_nt(rpat[1], sel[4])
        block = own[X0] * mask[4]
        own[X0] = block
        put_both(xaa_l, xaa_r, block)

        def three(slot):
            x = recs[slot]
            high = x.astype(BF16)
            rest = x - high.astype(F32)
            mid = rest.astype(BF16)
            low = (rest - mid.astype(F32)).astype(BF16)
            rows = pl.ds(pl.multiple_of(slot * N, N), N)
            split[rows, 0:FEAT] = high
            split[rows, FEAT : 2 * FEAT] = mid
            split[rows, 2 * FEAT : 3 * FEAT] = low

        three(4)
        lax.fori_loop(0, 4, mask_slot, 0)

        for j in range(RCH):
            arrive(recs.at[NEAR, rrows(j)], rec_s.at[3, j], rec_r.at[NEAR, j])
            send(recs.at[NEAR, rrows(j)], recs.at[FAR, rrows(j)], rec_s.at[3, j], rec_r.at[FAR, j], ahead)
        arrive(pats.at[NEAR], pat_s.at[3], pat_r.at[NEAR])
        send(pats.at[NEAR], pats.at[FAR], pat_s.at[3], pat_r.at[FAR], ahead)
        three(NEAR)
        for slot in (WEST, EAST, FAR):
            for j in range(RCH):
                arrive(recs.at[slot, rrows(j)], rec_s.at[3, j], rec_r.at[slot, j])
            three(slot)

        parts = dot(hot[...], split[...])
        migrated = (parts[:, 0:FEAT] + parts[:, FEAT : 2 * FEAT]) + parts[:, 2 * FEAT : 3 * FEAT]
        migs[4] = migrated
        for j in range(RCH):
            for way in (2, 0, 1):
                device, theirs = direct[way]
                send(migs.at[4, rrows(j)], migs.at[theirs, rrows(j)], mig_s.at[way, j], mig_rs.at[theirs, j], device)
        mig_copy = pltpu.make_async_copy(migs.at[4], mig_out, out_s.at[5])
        mig_copy.start()

        def put_mig(slot):
            high, low = halves(migs[slot])
            mig_l[slot, :, 0:FEAT] = high
            mig_l[slot, :, FEAT : 2 * FEAT] = high
            mig_l[slot, :, 2 * FEAT : 3 * FEAT] = low
            mig_r[slot, :, 0:FEAT] = high
            mig_r[slot, :, FEAT : 2 * FEAT] = low
            mig_r[slot, :, 2 * FEAT : 3 * FEAT] = high

        put_mig(4)
        put_left(eaa, dot_nt(mig_l[4], mig_r[4]) * coupling * dot_nt(rpat[0], sel[4]))

        for j in range(RCH):
            arrive(migs.at[NEAR, rrows(j)], mig_s.at[3, j], mig_rs.at[NEAR, j])
            send(migs.at[NEAR, rrows(j)], migs.at[FAR, rrows(j)], mig_s.at[3, j], mig_rs.at[FAR, j], ahead)

        def spread(kind):
            for j in range(CH):
                for way in (2, 0, 1):
                    device, theirs = direct[way]
                    send(
                        own.at[kind, crows(j)], diag.at[kind, theirs, crows(j)],
                        dia_s.at[kind, way, j], dia_r.at[kind, theirs, j], device,
                    )

        def take(kind, slot):
            def one(j, carry):
                rows = pl.ds(pl.multiple_of(j * CROWS, CROWS), CROWS)
                arrive(diag.at[kind, slot, rows], dia_s.at[kind, 3, j], dia_r.at[kind, slot, j])
                return carry

            lax.fori_loop(0, CH, one, 0)

        def forward(kind):
            for j in range(CH):
                arrive(diag.at[kind, NEAR, crows(j)], dia_s.at[kind, 3, j], dia_r.at[kind, NEAR, j])
                send(
                    diag.at[kind, NEAR, crows(j)], diag.at[kind, FAR, crows(j)],
                    dia_s.at[kind, 3, j], dia_r.at[kind, FAR, j], ahead,
                )

        spread(X0)

        def couple(slot):
            put_mig(slot)
            put_left(eab.at[slot], dot_nt(mig_l[4], mig_r[slot]) * coupling * dot_nt(rpat[0], sel[slot]))
            put_left(eba.at[slot], dot_nt(mig_l[slot], mig_r[4]) * coupling * dot_nt(sel[slot], rpat[0]))
            theirs = dot_nt(dot(spread_s, pats[slot].astype(BF16)).astype(BF16), sel[4])
            put_left(ebb.at[slot], dot_nt(mig_l[slot], mig_r[slot]) * coupling * theirs)

        def arrive_mig(slot):
            arrive(pats.at[slot], pat_s.at[3], pat_r.at[slot])
            for j in range(RCH):
                arrive(migs.at[slot, rrows(j)], mig_s.at[3, j], mig_rs.at[slot, j])

        def take_opp(slot):
            arrive(opp.at[slot], opp_s.at[slot], opp_r.at[slot])
            block = opp[slot] * mask[slot + 5]
            xba[slot] = block
            put_both(xba_l.at[slot], xba_r.at[slot], block)

        def couple_side(slot, carry):
            arrive_mig(slot)
            couple(slot)
            take_opp(slot)
            own[P1] += dot(eab[slot], xba_r[slot])
            return carry

        own[P1] = own[X0] + dot(eaa[...], xaa_r[...])
        lax.fori_loop(0, 2, couple_side, 0)
        couple(NEAR)
        take_opp(NEAR)
        own[P1] += dot(eab[NEAR], xba_r[NEAR])
        arrive_mig(FAR)
        couple(FAR)
        take_opp(FAR)
        block = (own[P1] + dot(eab[FAR], xba_r[FAR])) * mask[4]
        own[P1] = block
        spread(P1)
        put_right(paa_r, block)

        def back_product(slot):
            block = xba[slot] + dot(ebb[slot], xba_r[slot]) + dot(eba[slot], xaa_r[...])
            put_right(pba_r.at[slot], block * mask[slot + 5])

        def first_diag(slot, carry):
            back_product(slot)
            own[X1] -= dot(xab_l[slot], pba_r[slot])
            return carry

        own[X1] = 2.0 * own[X0] - dot(xaa_l[...], paa_r[...])
        lax.fori_loop(0, 4, first_diag, 0)
        block = own[X1] * mask[4]
        own[X1] = block
        spread(X1)
        put_both(x1aa_l, xaa_r, block)

        forward(X0)
        own[P2] = block + dot(eaa[...], xaa_r[...])

        def take_x0(slot):
            put_both(xbb_l.at[slot], xbb_r.at[slot], diag[X0, slot])

        def next_back(slot):
            take_x0(slot)
            block = 2.0 * xba[slot] - dot(xbb_l[slot], pba_r[slot]) - dot(xba_l[slot], paa_r[...])
            block = block * mask[slot + 5]
            xba[slot] = block
            put_right(xba_r.at[slot], block)
            own[P2] += dot(eab[slot], xba_r[slot])

        def next_side(slot, carry):
            take(X0, slot)
            next_back(slot)
            return carry

        lax.fori_loop(0, 2, next_side, 0)
        next_back(NEAR)
        take(X0, FAR)
        next_back(FAR)
        block = own[P2] * mask[4]
        own[P2] = block
        spread(P2)
        put_right(paa_r, block)

        outs[4] = 2.0 * own[X1] - dot(x1aa_l[...], paa_r[...])

        def ahead_product(slot, carry):
            block = xab[slot] + dot(eaa[...], xab_r[slot]) + dot(eab[slot], xbb_r[slot])
            put_right(pab_r.at[slot], block * mask[slot])
            xab[slot] = 2.0 * xab[slot] - dot(xaa_l[...], pab_r[slot])
            back_product(slot)
            return carry

        lax.fori_loop(0, 4, ahead_product, 0)

        def first_ahead(slot):
            put_right(pbb_r.at[slot], diag[P1, slot])
            block = (xab[slot] - dot(xab_l[slot], pbb_r[slot])) * mask[slot]
            xab[slot] = block
            put_both(xab_l.at[slot], xab_r.at[slot], block)
            outs[4] -= dot(xab_l[slot], pba_r[slot])

        def first_side(slot, carry):
            take(P1, slot)
            first_ahead(slot)
            return carry

        forward(P1)
        lax.fori_loop(0, 2, first_side, 0)
        first_ahead(NEAR)
        take(P1, FAR)
        first_ahead(FAR)
        outs[4] = outs[4] * mask[4]
        out_copies = [pltpu.make_async_copy(outs.at[4], inv_out.at[:, 0:N], out_s.at[4])]
        out_copies[0].start()

        def second_product(slot):
            put_right(xbb_r.at[slot], diag[X1, slot])
            block = xab[slot] + dot(eaa[...], xab_r[slot]) + dot(eab[slot], xbb_r[slot])
            put_right(pab_r.at[slot], block * mask[slot])
            xab[slot] = 2.0 * xab[slot] - dot(x1aa_l[...], pab_r[slot])

        def second_side(slot, carry):
            take(X1, slot)
            second_product(slot)
            return carry

        forward(X1)
        lax.fori_loop(0, 2, second_side, 0)
        second_product(NEAR)
        take(X1, FAR)
        second_product(FAR)

        def finish(slot):
            put_right(pbb_r.at[slot], diag[P2, slot])
            outs[slot] = (xab[slot] - dot(xab_l[slot], pbb_r[slot])) * mask[slot]
            copy = pltpu.make_async_copy(outs.at[slot], inv_out.at[:, cols(group[slot])], out_s.at[slot])
            copy.start()
            out_copies.append(copy)

        forward(P2)
        take(P2, WEST)
        finish(WEST)
        take(P2, EAST)
        finish(EAST)
        finish(NEAR)
        take(P2, FAR)
        finish(FAR)

        for copy in sends:
            copy.wait_send()
        mig_copy.wait()
        for copy in out_copies:
            copy.wait()

    return kernel


def solution(mesh):
    n_row, n_col = mesh.shape["row"], mesh.shape["col"]
    coupling = COUPLE_BASE / math.sqrt(5 * FEAT * N)
    vmem = pl.BlockSpec(memory_space=pltpu.VMEM)
    hbm = pl.BlockSpec(memory_space=pl.ANY)
    dma = pltpu.SemaphoreType.DMA

    def f32(*shape):
        return pltpu.VMEM(shape, F32)

    def bf16(*shape):
        return pltpu.VMEM(shape, BF16)

    left = bf16(N, 3 * N)
    left4 = bf16(4, N, 3 * N)
    right = bf16(3 * N, N)
    right4 = bf16(4, 3 * N, N)

    def body(records, move_face, move_slot, pattern_s, pattern_x, start_inverse):
        return pl.pallas_call(
            make_kernel(n_row, n_col, coupling),
            out_shape=(
                jax.ShapeDtypeStruct((N, FEAT), F32),
                jax.ShapeDtypeStruct((N, 5 * N), F32),
            ),
            in_specs=[hbm, vmem, vmem, vmem, vmem, hbm],
            out_specs=(hbm, hbm),
            scratch_shapes=[
                f32(5, N, FEAT), f32(5, 8, 128), f32(5, N, FEAT), f32(4, N, N), f32(4, 4, N, N), f32(4, N, N),
                f32(4, N, N), f32(4, N, N), f32(5, N, N),
                bf16(N, 5 * N), bf16(5 * N, 3 * FEAT), bf16(5, N, 3 * FEAT), bf16(5, N, 3 * FEAT),
                bf16(2, N, 128), bf16(5, N, 128), f32(9, N, N),
                left, left4, left4, left4,
                left, left, left4, left4, left4,
                right, right4, right4, right4, right, right4, right4, right4,
                dma((6,)), dma((4, RCH)), dma((4, RCH)), dma((4,)), dma((4,)), dma((4, RCH)), dma((4, RCH)),
                dma((4,)), dma((4,)), dma((4, 4, CH)), dma((4, 4, CH)), dma((6,)),
            ],
            compiler_params=pltpu.CompilerParams(
                collective_id=0, has_side_effects=True, vmem_limit_bytes=56 << 20
            ),
            cost_estimate=pl.CostEstimate(flops=8 * 10**9, bytes_accessed=3 * 2**20, transcendentals=0),
            name="hotelling",
        )(
            records,
            move_face.reshape(1, N),
            move_slot.reshape(1, N),
            pattern_s,
            pattern_x,
            start_inverse,
        )

    split = P(("row", "col"))
    wide = P(("row", "col"), None)
    return jax.shard_map(
        body,
        mesh=mesh,
        in_specs=(wide, split, split, wide, wide, wide),
        out_specs=(wide, wide),
        check_vma=False,
    )
```

```python
import math

import jax
import jax.numpy as jnp
from jax import lax
from jax.experimental import pallas as pl
from jax.experimental.pallas import tpu as pltpu
from jax.sharding import PartitionSpec as P

BLK = 64
COUPLE_BASE = 0.2
F32 = jnp.float32
BF16 = jnp.bfloat16
MESH = pl.DeviceIdType.MESH

N = 256
FEAT = 128
CH = 4
CROWS = N // CH
WEST, EAST, NEAR, FAR = 0, 1, 2, 3
X0, P1, X1, P2 = 0, 1, 2, 3
RCH = 2
RROWS = N // RCH
DETOUR = {X0: (0, 1), P1: (0, 1), X1: (0, 1), P2: ()}
RELAY = 4


def dot(a, b):
    return jnp.dot(a, b, preferred_element_type=F32)


def dot_nt(a, b):
    return lax.dot_general(a, b, (((1,), (1,)), ((), ())), preferred_element_type=F32)


def halves(x):
    high = x.astype(BF16)
    return high, (x - high.astype(F32)).astype(BF16)


def put_left(ref, x):
    high, low = halves(x)
    ref[:, 0:N] = high
    ref[:, N : 2 * N] = high
    ref[:, 2 * N : 3 * N] = low


def put_right(ref, x):
    high, low = halves(x)
    ref[0:N, :] = high
    ref[N : 2 * N, :] = low
    ref[2 * N : 3 * N, :] = high


def put_both(left, right, x):
    high, low = halves(x)
    left[:, 0:N] = high
    left[:, N : 2 * N] = high
    left[:, 2 * N : 3 * N] = low
    right[0:N, :] = high
    right[N : 2 * N, :] = low
    right[2 * N : 3 * N, :] = high


def make_kernel(n_row, n_col, coupling):
    def kernel(
        rec_hbm, face_ref, slot_ref, ps_ref, px_ref, x0_hbm,
        mig_out, inv_out,
        recs, pats, migs, opp, diag, own, xab, xba, outs,
        hot, split, mig_l, mig_r, rpat, sel, mask,
        eaa, eab, eba, ebb,
        xaa_l, x1aa_l, xab_l, xba_l, xbb_l,
        xaa_r, xab_r, xba_r, xbb_r, paa_r, pab_r, pba_r, pbb_r,
        loc, rec_s, rec_r, pat_s, pat_r, mig_s, mig_rs, opp_s, opp_r, dia_s, dia_r, out_s,
    ):
        r = lax.axis_index("row")
        c = lax.axis_index("col")
        odd = r % 2
        s = 1 - 2 * odd
        west = (r, (c + n_col - 1) % n_col)
        east = (r, (c + 1) % n_col)
        near = ((r + s + n_row) % n_row, c)
        far = ((r - s + n_row) % n_row, c)
        ahead = ((r + 2 * s + n_row) % n_row, c)
        behind = ((r - 2 * s + n_row) % n_row, c)
        group = (3, 4, 2 - odd, 1 + odd)
        direct = ((west, EAST), (east, WEST), (near, NEAR))
        at_first, at_last = c % 8 == 0, c % 8 == 7
        is_relay = (c % 8 == 2) | (c % 8 == 5)
        back2, on2 = (r, (c + n_col - 2) % n_col), (r, (c + 2) % n_col)
        back3, on3 = (r, (c + n_col - 3) % n_col), (r, (c + 3) % n_col)
        detour = (
            ((r, jnp.where(at_first, on2[1], west[1])), jnp.where(at_first, RELAY, EAST)),
            ((r, jnp.where(at_last, back2[1], east[1])), jnp.where(at_last, RELAY, WEST)),
        )
        forth = c % 2 == 1
        goal = (r, jnp.where(forth, on3[1], back3[1]))
        goal_slot = jnp.where(forth, WEST, EAST)

        def cols(q):
            return pl.ds(pl.multiple_of(q * N, N), N)

        local = []

        def fetch(src, dst):
            copy = pltpu.make_async_copy(src, dst, loc.at[len(local)])
            copy.start()
            local.append(copy)

        fetch(rec_hbm, recs.at[4])
        fetch(x0_hbm.at[:, 0:N], own.at[X0])
        for slot in range(4):
            fetch(x0_hbm.at[:, cols(group[slot])], xab.at[slot])

        pats[4] = jnp.zeros((8, 128), F32)
        pats[4, 0:4, 0:20] = jnp.where(ps_ref[...] > 0, 1.0, 0.0).astype(F32)
        pats[4, 4:8, 0:20] = jnp.where(px_ref[...] > 0, 1.0, 0.0).astype(F32)

        barrier = pltpu.get_barrier_semaphore()
        for other in (west, east, near, far, ahead, behind, back2, on2, back3, on3):
            pl.semaphore_signal(barrier, inc=1, device_id=other, device_id_type=MESH)
        pl.semaphore_wait(barrier, 10)

        def send(src, dst, ssem, rsem, device):
            copy = pltpu.make_async_remote_copy(
                src_ref=src, dst_ref=dst, send_sem=ssem, recv_sem=rsem, device_id=device, device_id_type=MESH
            )
            copy.start()

        def arrive(dst, ssem, rsem):
            pltpu.make_async_remote_copy(
                src_ref=dst, dst_ref=dst, send_sem=ssem, recv_sem=rsem, device_id=near, device_id_type=MESH
            ).wait_recv()

        def sent(src, ssem):
            pltpu.make_async_remote_copy(
                src_ref=src, dst_ref=src, send_sem=ssem, recv_sem=loc.at[0], device_id=near, device_id_type=MESH
            ).wait_send()

        def rrows(j):
            return pl.ds(j * RROWS, RROWS)

        def crows(j):
            return pl.ds(pl.multiple_of(j * CROWS, CROWS), CROWS)

        relayed = []

        def relay(src, dst, ssem, here, there):
            copy = pltpu.make_async_remote_copy(
                src_ref=src, dst_ref=dst, send_sem=ssem, recv_sem=there, device_id=goal, device_id_type=MESH
            )
            relayed.append(copy)

            @pl.when(is_relay)
            def _():
                arrive(src, ssem, here)
                copy.start()

        for j in range(RCH):
            for way in (2, 0, 1):
                device, theirs = direct[way]
                send(rec_hbm.at[rrows(j)], recs.at[theirs, rrows(j)], rec_s.at[way, j], rec_r.at[theirs, j], device)
        for way in (2, 0, 1):
            device, theirs = direct[way]
            send(pats.at[4], pats.at[theirs], pat_s.at[way], pat_r.at[theirs], device)
        for slot, (device, theirs) in ((FAR, (far, FAR)), (NEAR, (near, NEAR)), (WEST, detour[0]), (EAST, detour[1])):
            send(x0_hbm.at[:, cols(group[slot])], opp.at[theirs], opp_s.at[slot], opp_r.at[theirs], device)

        place = face_ref[...] * N + slot_ref[...]
        place = jnp.transpose(jnp.broadcast_to(place.astype(F32), (N, N)))
        lane = lax.broadcasted_iota(jnp.int32, (N, N), 1).astype(F32)
        for slot in range(5):
            q = 0 if slot == 4 else group[slot]
            first = (q * N * jnp.ones((1, 1), jnp.int32)).astype(F32)
            hot[:, slot * N : (slot + 1) * N] = jnp.where(place == lane + first, 1.0, 0.0).astype(BF16)

        row8 = lax.broadcasted_iota(jnp.int32, (N, 8), 0) // BLK
        col8 = lax.broadcasted_iota(jnp.int32, (N, 8), 1)
        spread_s = jnp.where(col8 == row8, 1.0, 0.0).astype(BF16)
        spread_x = jnp.where(col8 == row8 + 4, 1.0, 0.0).astype(BF16)
        row128 = lax.broadcasted_iota(jnp.int32, (N, 128), 0) // BLK
        col128 = lax.broadcasted_iota(jnp.int32, (N, 128), 1)
        for slot in range(5):
            q = 0 if slot == 4 else group[slot]
            sel[slot] = jnp.where(col128 == row128 + q * 4, 1.0, 0.0).astype(BF16)
        mine = pats[4].astype(BF16)
        rpat[0] = dot(spread_s, mine).astype(BF16)
        rpat[1] = dot(spread_x, mine).astype(BF16)

        for copy in local:
            copy.wait()

        def mask_slot(slot, carry):
            mask[slot] = dot_nt(rpat[1], sel[slot])
            mask[slot + 5] = dot_nt(sel[slot], rpat[1])
            block = xab[slot] * mask[slot]
            xab[slot] = block
            put_both(xab_l.at[slot], xab_r.at[slot], block)
            return carry

        mask[4] = dot_nt(rpat[1], sel[4])
        block = own[X0] * mask[4]
        own[X0] = block
        put_both(xaa_l, xaa_r, block)

        def three(slot):
            x = recs[slot]
            high = x.astype(BF16)
            rest = x - high.astype(F32)
            mid = rest.astype(BF16)
            low = (rest - mid.astype(F32)).astype(BF16)
            rows = pl.ds(pl.multiple_of(slot * N, N), N)
            split[rows, 0:FEAT] = high
            split[rows, FEAT : 2 * FEAT] = mid
            split[rows, 2 * FEAT : 3 * FEAT] = low

        three(4)
        lax.fori_loop(0, 4, mask_slot, 0)

        for j in range(RCH):
            arrive(recs.at[NEAR, rrows(j)], rec_s.at[3, j], rec_r.at[NEAR, j])
            send(recs.at[NEAR, rrows(j)], recs.at[FAR, rrows(j)], rec_s.at[3, j], rec_r.at[FAR, j], ahead)
        arrive(pats.at[NEAR], pat_s.at[3], pat_r.at[NEAR])
        send(pats.at[NEAR], pats.at[FAR], pat_s.at[3], pat_r.at[FAR], ahead)
        three(NEAR)
        for slot in (WEST, EAST, FAR):
            for j in range(RCH):
                arrive(recs.at[slot, rrows(j)], rec_s.at[3, j], rec_r.at[slot, j])
            three(slot)

        parts = dot(hot[...], split[...])
        migrated = (parts[:, 0:FEAT] + parts[:, FEAT : 2 * FEAT]) + parts[:, 2 * FEAT : 3 * FEAT]
        migs[4] = migrated
        for j in range(RCH):
            for way in (2, 0, 1):
                device, theirs = direct[way]
                send(migs.at[4, rrows(j)], migs.at[theirs, rrows(j)], mig_s.at[way, j], mig_rs.at[theirs, j], device)
        mig_copy = pltpu.make_async_copy(migs.at[4], mig_out, out_s.at[5])
        mig_copy.start()

        def put_mig(slot):
            high, low = halves(migs[slot])
            mig_l[slot, :, 0:FEAT] = high
            mig_l[slot, :, FEAT : 2 * FEAT] = high
            mig_l[slot, :, 2 * FEAT : 3 * FEAT] = low
            mig_r[slot, :, 0:FEAT] = high
            mig_r[slot, :, FEAT : 2 * FEAT] = low
            mig_r[slot, :, 2 * FEAT : 3 * FEAT] = high

        relay(opp.at[RELAY], opp.at[goal_slot], opp_s.at[RELAY], opp_r.at[RELAY], opp_r.at[goal_slot])

        put_mig(4)
        put_left(eaa, dot_nt(mig_l[4], mig_r[4]) * coupling * dot_nt(rpat[0], sel[4]))

        for j in range(RCH):
            arrive(migs.at[NEAR, rrows(j)], mig_s.at[3, j], mig_rs.at[NEAR, j])
            send(migs.at[NEAR, rrows(j)], migs.at[FAR, rrows(j)], mig_s.at[3, j], mig_rs.at[FAR, j], ahead)

        def spread(kind):
            for j in range(CH):
                for way in (2, 0, 1):
                    device, theirs = detour[way] if way < 2 and j in DETOUR[kind] else direct[way]
                    send(
                        own.at[kind, crows(j)], diag.at[kind, theirs, crows(j)],
                        dia_s.at[kind, way, j], dia_r.at[kind, theirs, j], device,
                    )

        def take(kind, slot):
            def one(j, carry):
                rows = pl.ds(pl.multiple_of(j * CROWS, CROWS), CROWS)
                arrive(diag.at[kind, slot, rows], dia_s.at[kind, 3, j], dia_r.at[kind, slot, j])
                return carry

            lax.fori_loop(0, CH, one, 0)

        def relay_diag(kind):
            for j in DETOUR[kind]:
                relay(
                    diag.at[kind, RELAY, crows(j)], diag.at[kind, goal_slot, crows(j)],
                    dia_s.at[kind, RELAY, j], dia_r.at[kind, RELAY, j], dia_r.at[kind, goal_slot, j],
                )

        def forward(kind, j):
            arrive(diag.at[kind, NEAR, crows(j)], dia_s.at[kind, 3, j], dia_r.at[kind, NEAR, j])
            send(
                diag.at[kind, NEAR, crows(j)], diag.at[kind, FAR, crows(j)],
                dia_s.at[kind, 3, j], dia_r.at[kind, FAR, j], ahead,
            )

        spread(X0)

        def couple(slot):
            put_mig(slot)
            put_left(eab.at[slot], dot_nt(mig_l[4], mig_r[slot]) * coupling * dot_nt(rpat[0], sel[slot]))

        def couple_back(slot):
            put_left(eba.at[slot], dot_nt(mig_l[slot], mig_r[4]) * coupling * dot_nt(sel[slot], rpat[0]))
            theirs = dot_nt(dot(spread_s, pats[slot].astype(BF16)).astype(BF16), sel[4])
            put_left(ebb.at[slot], dot_nt(mig_l[slot], mig_r[slot]) * coupling * theirs)

        def arrive_mig(slot):
            arrive(pats.at[slot], pat_s.at[3], pat_r.at[slot])
            for j in range(RCH):
                arrive(migs.at[slot, rrows(j)], mig_s.at[3, j], mig_rs.at[slot, j])

        def take_opp(slot):
            arrive(opp.at[slot], opp_s.at[slot], opp_r.at[slot])
            block = opp[slot] * mask[slot + 5]
            xba[slot] = block
            put_both(xba_l.at[slot], xba_r.at[slot], block)

        def couple_side(slot, carry):
            arrive_mig(slot)
            couple(slot)
            take_opp(slot)
            own[P1] += dot(eab[slot], xba_r[slot])
            return carry

        own[P1] = own[X0] + dot(eaa[...], xaa_r[...])
        lax.fori_loop(0, 2, couple_side, 0)
        couple(NEAR)
        take_opp(NEAR)
        own[P1] += dot(eab[NEAR], xba_r[NEAR])
        arrive_mig(FAR)
        couple(FAR)
        take_opp(FAR)
        block = (own[P1] + dot(eab[FAR], xba_r[FAR])) * mask[4]
        own[P1] = block
        spread(P1)
        put_right(paa_r, block)

        def back_product(slot):
            block = xba[slot] + dot(ebb[slot], xba_r[slot]) + dot(eba[slot], xaa_r[...])
            put_right(pba_r.at[slot], block * mask[slot + 5])

        def first_diag(slot, carry):
            couple_back(slot)
            back_product(slot)
            own[X1] -= dot(xab_l[slot], pba_r[slot])
            forward(X0, slot)
            return carry

        own[X1] = 2.0 * own[X0] - dot(xaa_l[...], paa_r[...])
        lax.fori_loop(0, 4, first_diag, 0)
        block = own[X1] * mask[4]
        own[X1] = block
        spread(X1)
        put_both(x1aa_l, xaa_r, block)

        relay_diag(X0)
        own[P2] = block + dot(eaa[...], xaa_r[...])

        def take_x0(slot):
            put_both(xbb_l.at[slot], xbb_r.at[slot], diag[X0, slot])

        def next_back(slot):
            take_x0(slot)
            block = 2.0 * xba[slot] - dot(xbb_l[slot], pba_r[slot]) - dot(xba_l[slot], paa_r[...])
            block = block * mask[slot + 5]
            xba[slot] = block
            put_right(xba_r.at[slot], block)
            own[P2] += dot(eab[slot], xba_r[slot])

        def next_side(slot, carry):
            take(X0, slot)
            next_back(slot)
            return carry

        lax.fori_loop(0, 2, next_side, 0)
        forward(P1, 0)
        next_back(NEAR)
        forward(P1, 1)
        take(X0, FAR)
        next_back(FAR)
        block = own[P2] * mask[4]
        own[P2] = block
        spread(P2)
        put_right(paa_r, block)

        forward(P1, 2)
        forward(P1, 3)
        relay_diag(P1)
        outs[4] = 2.0 * own[X1] - dot(x1aa_l[...], paa_r[...])

        def ahead_product(slot, carry):
            block = xab[slot] + dot(eaa[...], xab_r[slot]) + dot(eab[slot], xbb_r[slot])
            put_right(pab_r.at[slot], block * mask[slot])
            xab[slot] = 2.0 * xab[slot] - dot(xaa_l[...], pab_r[slot])
            back_product(slot)
            forward(X1, slot)
            return carry

        lax.fori_loop(0, 4, ahead_product, 0)
        relay_diag(X1)

        def first_ahead(slot):
            put_right(pbb_r.at[slot], diag[P1, slot])
            block = (xab[slot] - dot(xab_l[slot], pbb_r[slot])) * mask[slot]
            xab[slot] = block
            put_both(xab_l.at[slot], xab_r.at[slot], block)
            outs[4] -= dot(xab_l[slot], pba_r[slot])

        def first_side(slot, carry):
            take(P1, slot)
            first_ahead(slot)
            return carry

        lax.fori_loop(0, 2, first_side, 0)
        first_ahead(NEAR)
        take(P1, FAR)
        first_ahead(FAR)
        outs[4] = outs[4] * mask[4]
        out_copies = [pltpu.make_async_copy(outs.at[4], inv_out.at[:, 0:N], out_s.at[4])]
        out_copies[0].start()

        def second_product(slot):
            put_right(xbb_r.at[slot], diag[X1, slot])
            block = xab[slot] + dot(eaa[...], xab_r[slot]) + dot(eab[slot], xbb_r[slot])
            put_right(pab_r.at[slot], block * mask[slot])
            xab[slot] = 2.0 * xab[slot] - dot(x1aa_l[...], pab_r[slot])

        def second_side(slot, carry):
            take(X1, slot)
            second_product(slot)
            return carry

        lax.fori_loop(0, 2, second_side, 0)
        forward(P2, 0)
        second_product(NEAR)
        forward(P2, 1)
        take(X1, FAR)
        forward(P2, 2)
        second_product(FAR)
        forward(P2, 3)

        def finish(slot):
            put_right(pbb_r.at[slot], diag[P2, slot])
            outs[slot] = (xab[slot] - dot(xab_l[slot], pbb_r[slot])) * mask[slot]
            copy = pltpu.make_async_copy(outs.at[slot], inv_out.at[:, cols(group[slot])], out_s.at[slot])
            copy.start()
            out_copies.append(copy)

        take(P2, WEST)
        finish(WEST)
        take(P2, EAST)
        finish(EAST)
        finish(NEAR)
        take(P2, FAR)
        finish(FAR)

        def sent_way(way, carry):
            sent(pats.at[4], pat_s.at[way])
            sent(opp.at[way], opp_s.at[way])
            for j in range(RCH):
                sent(recs.at[4, rrows(j)], rec_s.at[way, j])
                sent(migs.at[4, rrows(j)], mig_s.at[way, j])

            def sent_kind(kind, carry):
                for j in range(CH):
                    sent(own.at[kind, crows(j)], dia_s.at[kind, way, j])
                return carry

            return lax.fori_loop(0, 4, sent_kind, carry)

        lax.fori_loop(0, 4, sent_way, 0)

        @pl.when(is_relay)
        def _():
            for copy in relayed:
                copy.wait_send()

        mig_copy.wait()
        for copy in out_copies:
            copy.wait()

    return kernel


def hand_over(mig_in, inv_in, mig_out, inv_out):
    mig_out[...] = mig_in[...]
    inv_out[...] = inv_in[...]


def solution(mesh):
    n_row, n_col = mesh.shape["row"], mesh.shape["col"]
    coupling = COUPLE_BASE / math.sqrt(5 * FEAT * N)
    vmem = pl.BlockSpec(memory_space=pltpu.VMEM)
    hbm = pl.BlockSpec(memory_space=pl.ANY)
    dma = pltpu.SemaphoreType.DMA

    def f32(*shape):
        return pltpu.VMEM(shape, F32)

    def bf16(*shape):
        return pltpu.VMEM(shape, BF16)

    left = bf16(N, 3 * N)
    left4 = bf16(4, N, 3 * N)
    right = bf16(3 * N, N)
    right4 = bf16(4, 3 * N, N)

    def body(records, move_face, move_slot, pattern_s, pattern_x, start_inverse):
        shapes = (jax.ShapeDtypeStruct((N, FEAT), F32), jax.ShapeDtypeStruct((N, 5 * N), F32))
        results = pl.pallas_call(
            make_kernel(n_row, n_col, coupling),
            out_shape=shapes,
            in_specs=[hbm, vmem, vmem, vmem, vmem, hbm],
            out_specs=(hbm, hbm),
            scratch_shapes=[
                f32(5, N, FEAT), f32(5, 8, 128), f32(5, N, FEAT), f32(5, N, N), f32(4, 5, N, N), f32(4, N, N),
                f32(4, N, N), f32(4, N, N), f32(5, N, N),
                bf16(N, 5 * N), bf16(5 * N, 3 * FEAT), bf16(5, N, 3 * FEAT), bf16(5, N, 3 * FEAT),
                bf16(2, N, 128), bf16(5, N, 128), f32(9, N, N),
                left, left4, left4, left4,
                left, left, left4, left4, left4,
                right, right4, right4, right4, right, right4, right4, right4,
                dma((6,)), dma((4, RCH)), dma((4, RCH)), dma((4,)), dma((4,)), dma((4, RCH)), dma((4, RCH)),
                dma((5,)), dma((5,)), dma((4, 5, CH)), dma((4, 5, CH)), dma((6,)),
            ],
            compiler_params=pltpu.CompilerParams(
                collective_id=0, has_side_effects=True, vmem_limit_bytes=56 << 20
            ),
            cost_estimate=pl.CostEstimate(flops=8 * 10**9, bytes_accessed=3 * 2**20, transcendentals=0),
            name="hotelling",
        )(
            records,
            move_face.reshape(1, N),
            move_slot.reshape(1, N),
            pattern_s,
            pattern_x,
            start_inverse,
        )
        return pl.pallas_call(
            hand_over,
            out_shape=shapes,
            in_specs=[vmem, vmem],
            out_specs=(vmem, vmem),
            name="hand_over",
        )(*results)

    split = P(("row", "col"))
    wide = P(("row", "col"), None)
    return jax.shard_map(
        body,
        mesh=mesh,
        in_specs=(wide, split, split, wide, wide, wide),
        out_specs=(wide, wide),
        check_vma=False,
    )
```

```python
import math

import jax
import jax.numpy as jnp
from jax import lax
from jax.experimental import pallas as pl
from jax.experimental.pallas import tpu as pltpu
from jax.sharding import PartitionSpec as P

BLK = 64
COUPLE_BASE = 0.2
F32 = jnp.float32
BF16 = jnp.bfloat16
MESH = pl.DeviceIdType.MESH

N = 256
FEAT = 128
CH = 4
CROWS = N // CH
WEST, EAST, NEAR, FAR = 0, 1, 2, 3
X0, P1, X1, P2 = 0, 1, 2, 3
RCH = 2
RROWS = N // RCH
DETOUR = {X0: (0, 1), P1: (0, 1), X1: (0, 1), P2: (0, 1)}
RELAY = 4


def dot(a, b):
    return jnp.dot(a, b, preferred_element_type=F32)


def dot_nt(a, b):
    return lax.dot_general(a, b, (((1,), (1,)), ((), ())), preferred_element_type=F32)


def halves(x):
    high = x.astype(BF16)
    return high, (x - high.astype(F32)).astype(BF16)


def put_left(ref, x):
    high, low = halves(x)
    ref[:, 0:N] = high
    ref[:, N : 2 * N] = high
    ref[:, 2 * N : 3 * N] = low


def put_right(ref, x):
    high, low = halves(x)
    ref[0:N, :] = high
    ref[N : 2 * N, :] = low
    ref[2 * N : 3 * N, :] = high


def put_both(left, right, x):
    high, low = halves(x)
    left[:, 0:N] = high
    left[:, N : 2 * N] = high
    left[:, 2 * N : 3 * N] = low
    right[0:N, :] = high
    right[N : 2 * N, :] = low
    right[2 * N : 3 * N, :] = high


def make_kernel(n_row, n_col, coupling):
    def kernel(
        rec_hbm, face_ref, slot_ref, ps_ref, px_ref, x0_hbm,
        mig_out, inv_out,
        recs, pats, migs, opp, diag, own, xab, xba, pab, outs,
        hot, split, mig_l, mig_r, rpat, sel, mask, link,
        eaa, eab, eba, ebb,
        xaa_l, x1aa_l, xab_l, xba_l, xbb_l,
        xaa_r, xab_r, xba_r, xbb_r, paa_r, pab_r, pba_r, pbb_r,
        loc, rec_s, rec_r, pat_s, pat_r, mig_s, mig_rs, opp_s, opp_r, dia_s, dia_r, out_s,
    ):
        r = lax.axis_index("row")
        c = lax.axis_index("col")
        odd = r % 2
        s = 1 - 2 * odd
        west = (r, (c + n_col - 1) % n_col)
        east = (r, (c + 1) % n_col)
        near = ((r + s + n_row) % n_row, c)
        far = ((r - s + n_row) % n_row, c)
        ahead = ((r + 2 * s + n_row) % n_row, c)
        behind = ((r - 2 * s + n_row) % n_row, c)
        group = (3, 4, 2 - odd, 1 + odd)
        direct = ((west, EAST), (east, WEST), (near, NEAR))
        at_first, at_last = c % 8 == 0, c % 8 == 7
        is_relay = (c % 8 == 2) | (c % 8 == 5)
        back2, on2 = (r, (c + n_col - 2) % n_col), (r, (c + 2) % n_col)
        back3, on3 = (r, (c + n_col - 3) % n_col), (r, (c + 3) % n_col)
        detour = (
            ((r, jnp.where(at_first, on2[1], west[1])), jnp.where(at_first, RELAY, EAST)),
            ((r, jnp.where(at_last, back2[1], east[1])), jnp.where(at_last, RELAY, WEST)),
        )
        forth = c % 2 == 1
        goal = (r, jnp.where(forth, on3[1], back3[1]))
        goal_slot = jnp.where(forth, WEST, EAST)

        def cols(q):
            return pl.ds(pl.multiple_of(q * N, N), N)

        local = []

        def fetch(src, dst):
            copy = pltpu.make_async_copy(src, dst, loc.at[len(local)])
            copy.start()
            local.append(copy)

        fetch(rec_hbm, recs.at[4])
        fetch(x0_hbm.at[:, 0:N], own.at[X0])
        for slot in range(4):
            fetch(x0_hbm.at[:, cols(group[slot])], xab.at[slot])

        pats[4] = jnp.zeros((8, 128), F32)
        pats[4, 0:4, 0:20] = jnp.where(ps_ref[...] > 0, 1.0, 0.0).astype(F32)
        pats[4, 4:8, 0:20] = jnp.where(px_ref[...] > 0, 1.0, 0.0).astype(F32)

        barrier = pltpu.get_barrier_semaphore()
        for other in (west, east, near, far, ahead, behind, back2, on2, back3, on3):
            pl.semaphore_signal(barrier, inc=1, device_id=other, device_id_type=MESH)
        pl.semaphore_wait(barrier, 10)

        def send(src, dst, ssem, rsem, device):
            copy = pltpu.make_async_remote_copy(
                src_ref=src, dst_ref=dst, send_sem=ssem, recv_sem=rsem, device_id=device, device_id_type=MESH
            )
            copy.start()

        def arrive(dst, ssem, rsem):
            pltpu.make_async_remote_copy(
                src_ref=dst, dst_ref=dst, send_sem=ssem, recv_sem=rsem, device_id=near, device_id_type=MESH
            ).wait_recv()

        def sent(src, ssem):
            pltpu.make_async_remote_copy(
                src_ref=src, dst_ref=src, send_sem=ssem, recv_sem=loc.at[0], device_id=near, device_id_type=MESH
            ).wait_send()

        def rrows(j):
            return pl.ds(j * RROWS, RROWS)

        def crows(j):
            return pl.ds(pl.multiple_of(j * CROWS, CROWS), CROWS)

        relayed = []

        def relay(src, dst, ssem, here, there):
            copy = pltpu.make_async_remote_copy(
                src_ref=src, dst_ref=dst, send_sem=ssem, recv_sem=there, device_id=goal, device_id_type=MESH
            )
            relayed.append(copy)

            @pl.when(is_relay)
            def _():
                arrive(src, ssem, here)
                copy.start()

        for j in range(RCH):
            for way in (2, 0, 1):
                device, theirs = direct[way]
                send(rec_hbm.at[rrows(j)], recs.at[theirs, rrows(j)], rec_s.at[way, j], rec_r.at[theirs, j], device)
        for way in (2, 0, 1):
            device, theirs = direct[way]
            send(pats.at[4], pats.at[theirs], pat_s.at[way], pat_r.at[theirs], device)
        place = face_ref[...] * N + slot_ref[...]
        place = jnp.transpose(jnp.broadcast_to(place.astype(F32), (N, N)))
        lane = lax.broadcasted_iota(jnp.int32, (N, N), 1).astype(F32)
        for slot in range(5):
            q = 0 if slot == 4 else group[slot]
            first = (q * N * jnp.ones((1, 1), jnp.int32)).astype(F32)
            hot[:, slot * N : (slot + 1) * N] = jnp.where(place == lane + first, 1.0, 0.0).astype(BF16)

        row8 = lax.broadcasted_iota(jnp.int32, (N, 8), 0) // BLK
        col8 = lax.broadcasted_iota(jnp.int32, (N, 8), 1)
        spread_s = jnp.where(col8 == row8, 1.0, 0.0).astype(BF16)
        spread_x = jnp.where(col8 == row8 + 4, 1.0, 0.0).astype(BF16)
        row128 = lax.broadcasted_iota(jnp.int32, (N, 128), 0) // BLK
        col128 = lax.broadcasted_iota(jnp.int32, (N, 128), 1)
        for slot in range(5):
            q = 0 if slot == 4 else group[slot]
            sel[slot] = jnp.where(col128 == row128 + q * 4, 1.0, 0.0).astype(BF16)
        mine = pats[4].astype(BF16)
        rpat[0] = dot(spread_s, mine).astype(BF16)
        rpat[1] = dot(spread_x, mine).astype(BF16)

        for j in range(RCH):
            sent(recs.at[4, rrows(j)], rec_s.at[2, j])
        for slot, (device, theirs) in ((FAR, (far, FAR)), (NEAR, (near, NEAR)), (WEST, detour[0]), (EAST, detour[1])):
            send(x0_hbm.at[:, cols(group[slot])], opp.at[theirs], opp_s.at[slot], opp_r.at[theirs], device)


        for copy in local:
            copy.wait()

        for slot in range(5):
            mask[slot] = dot_nt(rpat[1], sel[slot])
            link[slot] = dot_nt(rpat[0], sel[slot]) * coupling
        for slot in range(4):
            mask[slot + 5] = dot_nt(sel[slot], rpat[1])
            link[slot + 5] = dot_nt(sel[slot], rpat[0]) * coupling
        for slot in range(4):
            block = xab[slot] * mask[slot]
            xab[slot] = block
            put_both(xab_l.at[slot], xab_r.at[slot], block)
        block = own[X0] * mask[4]
        own[X0] = block
        put_both(xaa_l, xaa_r, block)

        def three(slot):
            x = recs[slot]
            high = x.astype(BF16)
            rest = x - high.astype(F32)
            mid = rest.astype(BF16)
            low = (rest - mid.astype(F32)).astype(BF16)
            rows = pl.ds(pl.multiple_of(slot * N, N), N)
            split[rows, 0:FEAT] = high
            split[rows, FEAT : 2 * FEAT] = mid
            split[rows, 2 * FEAT : 3 * FEAT] = low

        three(4)

        for j in range(RCH):
            arrive(recs.at[NEAR, rrows(j)], rec_s.at[3, j], rec_r.at[NEAR, j])
            send(recs.at[NEAR, rrows(j)], recs.at[FAR, rrows(j)], rec_s.at[3, j], rec_r.at[FAR, j], ahead)
        arrive(pats.at[NEAR], pat_s.at[3], pat_r.at[NEAR])
        send(pats.at[NEAR], pats.at[FAR], pat_s.at[3], pat_r.at[FAR], ahead)
        three(NEAR)
        for slot in (WEST, EAST, FAR):
            for j in range(RCH):
                arrive(recs.at[slot, rrows(j)], rec_s.at[3, j], rec_r.at[slot, j])
            three(slot)
            arrive(pats.at[slot], pat_s.at[3], pat_r.at[slot])

        def spread(kind):
            for j in range(CH):
                for way in (2, 0, 1):
                    device, theirs = detour[way] if way < 2 and j in DETOUR[kind] else direct[way]
                    send(
                        own.at[kind, crows(j)], diag.at[kind, theirs, crows(j)],
                        dia_s.at[kind, way, j], dia_r.at[kind, theirs, j], device,
                    )

        def relay_diag(kind):
            for j in DETOUR[kind]:
                relay(
                    diag.at[kind, RELAY, crows(j)], diag.at[kind, goal_slot, crows(j)],
                    dia_s.at[kind, RELAY, j], dia_r.at[kind, RELAY, j], dia_r.at[kind, goal_slot, j],
                )

        def take(kind, slot):
            for j in range(CH):
                arrive(diag.at[kind, slot, crows(j)], dia_s.at[kind, 3, j], dia_r.at[kind, slot, j])

        def forward(kind, j):
            arrive(diag.at[kind, NEAR, crows(j)], dia_s.at[kind, 3, j], dia_r.at[kind, NEAR, j])
            send(
                diag.at[kind, NEAR, crows(j)], diag.at[kind, FAR, crows(j)],
                dia_s.at[kind, 3, j], dia_r.at[kind, FAR, j], ahead,
            )

        def forward_all(kind):
            for j in range(CH):
                forward(kind, j)

        parts = dot(hot[...], split[...])
        migrated = (parts[:, 0:FEAT] + parts[:, FEAT : 2 * FEAT]) + parts[:, 2 * FEAT : 3 * FEAT]
        migs[4] = migrated
        for j in range(RCH):
            for way in (2, 0, 1):
                device, theirs = direct[way]
                send(migs.at[4, rrows(j)], migs.at[theirs, rrows(j)], mig_s.at[way, j], mig_rs.at[theirs, j], device)
        mig_copy = pltpu.make_async_copy(migs.at[4], mig_out, out_s.at[5])
        mig_copy.start()

        def put_mig(slot):
            high, low = halves(migs[slot])
            mig_l[slot, :, 0:FEAT] = high
            mig_l[slot, :, FEAT : 2 * FEAT] = high
            mig_l[slot, :, 2 * FEAT : 3 * FEAT] = low
            mig_r[slot, :, 0:FEAT] = high
            mig_r[slot, :, FEAT : 2 * FEAT] = low
            mig_r[slot, :, 2 * FEAT : 3 * FEAT] = high

        relay(opp.at[RELAY], opp.at[goal_slot], opp_s.at[RELAY], opp_r.at[RELAY], opp_r.at[goal_slot])

        for slot in range(4):
            link[slot + 9] = dot_nt(dot(spread_s, pats[slot].astype(BF16)).astype(BF16), sel[4]) * coupling
        put_mig(4)
        put_left(eaa, dot_nt(mig_l[4], mig_r[4]) * link[4])
        own[P1] = own[X0] + dot(eaa[...], xaa_r[...])
        for slot in range(4):
            pab[slot] = xab[slot] + dot(eaa[...], xab_r[slot])

        for j in range(RCH):
            arrive(migs.at[NEAR, rrows(j)], mig_s.at[3, j], mig_rs.at[NEAR, j])
            send(migs.at[NEAR, rrows(j)], migs.at[FAR, rrows(j)], mig_s.at[3, j], mig_rs.at[FAR, j], ahead)
        spread(X0)

        def couple(*slots):
            for slot in slots:
                put_mig(slot)
            for slot in slots:
                put_left(eab.at[slot], dot_nt(mig_l[4], mig_r[slot]) * link[slot])

        def couple_back(*slots):
            for slot in slots:
                put_left(eba.at[slot], dot_nt(mig_l[slot], mig_r[4]) * link[slot + 5])
                put_left(ebb.at[slot], dot_nt(mig_l[slot], mig_r[slot]) * link[slot + 9])

        def arrive_mig(slot):
            for j in range(RCH):
                arrive(migs.at[slot, rrows(j)], mig_s.at[3, j], mig_rs.at[slot, j])

        def take_opp(*slots):
            for slot in slots:
                arrive(opp.at[slot], opp_s.at[slot], opp_r.at[slot])
            for slot in slots:
                block = opp[slot] * mask[slot + 5]
                xba[slot] = block
                put_both(xba_l.at[slot], xba_r.at[slot], block)

        def back_product(*slots):
            for slot in slots:
                block = xba[slot] + dot(ebb[slot], xba_r[slot]) + dot(eba[slot], xaa_r[...])
                put_right(pba_r.at[slot], block * mask[slot + 5])

        arrive_mig(WEST)
        arrive_mig(EAST)
        couple(WEST, EAST, NEAR)
        take_opp(WEST, EAST, NEAR, FAR)
        own[P1] = own[P1] + dot(eab[WEST], xba_r[WEST]) + dot(eab[EAST], xba_r[EAST]) + dot(eab[NEAR], xba_r[NEAR])
        couple_back(WEST, EAST)
        back_product(WEST, EAST)
        own[X1] = 2.0 * own[X0] - dot(xab_l[WEST], pba_r[WEST]) - dot(xab_l[EAST], pba_r[EAST])

        relay_diag(X0)
        arrive_mig(FAR)
        couple(FAR)
        block = (own[P1] + dot(eab[FAR], xba_r[FAR])) * mask[4]
        own[P1] = block
        spread(P1)
        put_right(paa_r, block)
        couple_back(NEAR, FAR)
        back_product(NEAR, FAR)
        block = own[X1] - dot(xab_l[NEAR], pba_r[NEAR]) - dot(xab_l[FAR], pba_r[FAR]) - dot(xaa_l[...], paa_r[...])
        block = block * mask[4]
        own[X1] = block
        spread(X1)
        put_both(x1aa_l, xaa_r, block)
        forward_all(X0)

        def next_back(*slots):
            for slot in slots:
                put_both(xbb_l.at[slot], xbb_r.at[slot], diag[X0, slot])
            for slot in slots:
                block = 2.0 * xba[slot] - dot(xbb_l[slot], pba_r[slot]) - dot(xba_l[slot], paa_r[...])
                block = block * mask[slot + 5]
                xba[slot] = block
                put_right(xba_r.at[slot], block)

        take(X0, WEST)
        take(X0, EAST)
        next_back(WEST, EAST, NEAR)
        own[P2] = (
            own[X1] + dot(eaa[...], xaa_r[...])
            + dot(eab[WEST], xba_r[WEST]) + dot(eab[EAST], xba_r[EAST]) + dot(eab[NEAR], xba_r[NEAR])
        )
        take(X0, FAR)
        next_back(FAR)
        block = (own[P2] + dot(eab[FAR], xba_r[FAR])) * mask[4]
        own[P2] = block
        spread(P2)
        put_right(paa_r, block)

        def ahead_product(*slots):
            for slot in slots:
                block = pab[slot] + dot(eab[slot], xbb_r[slot])
                put_right(pab_r.at[slot], block * mask[slot])
            for slot in slots:
                xab[slot] = 2.0 * xab[slot] - dot(xaa_l[...], pab_r[slot])

        relay_diag(P1)
        forward_all(P1)
        ahead_product(WEST, EAST, NEAR, FAR)
        back_product(WEST, EAST, NEAR, FAR)
        outs[4] = 2.0 * own[X1] - dot(x1aa_l[...], paa_r[...])
        relay_diag(X1)
        forward_all(X1)

        def first_ahead(*slots):
            for slot in slots:
                put_right(pbb_r.at[slot], diag[P1, slot])
            for slot in slots:
                block = (xab[slot] - dot(xab_l[slot], pbb_r[slot])) * mask[slot]
                xab[slot] = block
                put_both(xab_l.at[slot], xab_r.at[slot], block)

        take(P1, WEST)
        take(P1, EAST)
        first_ahead(WEST, EAST, NEAR)
        take(P1, FAR)
        first_ahead(FAR)
        block = outs[4] - dot(xab_l[WEST], pba_r[WEST]) - dot(xab_l[EAST], pba_r[EAST])
        outs[4] = (block - dot(xab_l[NEAR], pba_r[NEAR]) - dot(xab_l[FAR], pba_r[FAR])) * mask[4]
        out_copies = [pltpu.make_async_copy(outs.at[4], inv_out.at[:, 0:N], out_s.at[4])]
        out_copies[0].start()

        def second_product(*slots):
            for slot in slots:
                put_right(xbb_r.at[slot], diag[X1, slot])
            for slot in slots:
                block = xab[slot] + dot(eaa[...], xab_r[slot]) + dot(eab[slot], xbb_r[slot])
                put_right(pab_r.at[slot], block * mask[slot])
            for slot in slots:
                xab[slot] = 2.0 * xab[slot] - dot(x1aa_l[...], pab_r[slot])

        take(X1, WEST)
        take(X1, EAST)
        second_product(WEST, EAST, NEAR)
        relay_diag(P2)
        forward_all(P2)
        take(X1, FAR)
        second_product(FAR)

        def finish(*slots):
            for slot in slots:
                put_right(pbb_r.at[slot], diag[P2, slot])
            for slot in slots:
                outs[slot] = (xab[slot] - dot(xab_l[slot], pbb_r[slot])) * mask[slot]
            for slot in slots:
                copy = pltpu.make_async_copy(outs.at[slot], inv_out.at[:, cols(group[slot])], out_s.at[slot])
                copy.start()
                out_copies.append(copy)

        take(P2, WEST)
        take(P2, EAST)
        finish(WEST, EAST, NEAR)
        take(P2, FAR)
        finish(FAR)

        def sent_diag(way):
            def sent_kind(kind, carry):
                for j in range(CH):
                    sent(own.at[kind, crows(j)], dia_s.at[kind, way, j])
                return carry

            lax.fori_loop(0, 4, sent_kind, 0)

        def sent_way(way, carry):
            sent(pats.at[4], pat_s.at[way])
            sent(opp.at[way], opp_s.at[way])
            for j in range(RCH):
                sent(migs.at[4, rrows(j)], mig_s.at[way, j])
            return carry

        lax.fori_loop(0, 4, sent_way, 0)
        for way in (0, 1, 3):
            for j in range(RCH):
                sent(recs.at[4, rrows(j)], rec_s.at[way, j])
        for way in range(4):
            sent_diag(way)

        @pl.when(is_relay)
        def _():
            for copy in relayed:
                copy.wait_send()

        mig_copy.wait()
        for copy in out_copies:
            copy.wait()

    return kernel


def hand_over(mig_in, inv_in, mig_out, inv_out):
    mig_out[...] = mig_in[...]
    inv_out[...] = inv_in[...]


def solution(mesh):
    n_row, n_col = mesh.shape["row"], mesh.shape["col"]
    coupling = COUPLE_BASE / math.sqrt(5 * FEAT * N)
    vmem = pl.BlockSpec(memory_space=pltpu.VMEM)
    hbm = pl.BlockSpec(memory_space=pl.ANY)
    dma = pltpu.SemaphoreType.DMA

    def f32(*shape):
        return pltpu.VMEM(shape, F32)

    def bf16(*shape):
        return pltpu.VMEM(shape, BF16)

    left = bf16(N, 3 * N)
    left4 = bf16(4, N, 3 * N)
    right = bf16(3 * N, N)
    right4 = bf16(4, 3 * N, N)

    def body(records, move_face, move_slot, pattern_s, pattern_x, start_inverse):
        shapes = (jax.ShapeDtypeStruct((N, FEAT), F32), jax.ShapeDtypeStruct((N, 5 * N), F32))
        results = pl.pallas_call(
            make_kernel(n_row, n_col, coupling),
            out_shape=shapes,
            in_specs=[hbm, vmem, vmem, vmem, vmem, hbm],
            out_specs=(hbm, hbm),
            scratch_shapes=[
                f32(5, N, FEAT), f32(5, 8, 128), f32(5, N, FEAT), f32(5, N, N), f32(4, 5, N, N), f32(4, N, N),
                f32(4, N, N), f32(4, N, N), f32(4, N, N), f32(5, N, N),
                bf16(N, 5 * N), bf16(5 * N, 3 * FEAT), bf16(5, N, 3 * FEAT), bf16(5, N, 3 * FEAT),
                bf16(2, N, 128), bf16(5, N, 128), f32(9, N, N), f32(13, N, N),
                left, left4, left4, left4,
                left, left, left4, left4, left4,
                right, right4, right4, right4, right, right4, right4, right4,
                dma((6,)), dma((4, RCH)), dma((4, RCH)), dma((4,)), dma((4,)), dma((4, RCH)), dma((4, RCH)),
                dma((5,)), dma((5,)), dma((4, 5, CH)), dma((4, 5, CH)), dma((6,)),
            ],
            compiler_params=pltpu.CompilerParams(
                collective_id=0, has_side_effects=True, vmem_limit_bytes=56 << 20
            ),
            cost_estimate=pl.CostEstimate(flops=8 * 10**9, bytes_accessed=3 * 2**20, transcendentals=0),
            name="hotelling",
        )(
            records,
            move_face.reshape(1, N),
            move_slot.reshape(1, N),
            pattern_s,
            pattern_x,
            start_inverse,
        )
        return pl.pallas_call(
            hand_over,
            out_shape=shapes,
            in_specs=[vmem, vmem],
            out_specs=(vmem, vmem),
            name="hand_over",
        )(*results)

    split = P(("row", "col"))
    wide = P(("row", "col"), None)
    return jax.shard_map(
        body,
        mesh=mesh,
        in_specs=(wide, split, split, wide, wide, wide),
        out_specs=(wide, wide),
        check_vma=False,
    )
```

```python
import math

import jax
import jax.numpy as jnp
from jax import lax
from jax.experimental import pallas as pl
from jax.experimental.pallas import tpu as pltpu
from jax.sharding import PartitionSpec as P

BLK = 64
COUPLE_BASE = 0.2
F32 = jnp.float32
BF16 = jnp.bfloat16
MESH = pl.DeviceIdType.MESH

N = 256
FEAT = 128
CH = 4
CROWS = N // CH
WEST, EAST, NEAR, FAR = 0, 1, 2, 3
X0, P1, X1, P2 = 0, 1, 2, 3
RCH = 2
RROWS = N // RCH
DETOUR = {X0: (0, 1), P1: (0, 1), X1: (0, 1), P2: (0,)}
RELAY = 4


def dot(a, b):
    return jnp.dot(a, b, preferred_element_type=F32)


def dot_nt(a, b):
    return lax.dot_general(a, b, (((1,), (1,)), ((), ())), preferred_element_type=F32)


def halves(x):
    high = x.astype(BF16)
    return high, (x - high.astype(F32)).astype(BF16)


def put_left(ref, x):
    high, low = halves(x)
    ref[:, 0:N] = high
    ref[:, N : 2 * N] = high
    ref[:, 2 * N : 3 * N] = low


def put_right(ref, x):
    high, low = halves(x)
    ref[0:N, :] = high
    ref[N : 2 * N, :] = low
    ref[2 * N : 3 * N, :] = high


def put_both(left, right, x):
    high, low = halves(x)
    left[:, 0:N] = high
    left[:, N : 2 * N] = high
    left[:, 2 * N : 3 * N] = low
    right[0:N, :] = high
    right[N : 2 * N, :] = low
    right[2 * N : 3 * N, :] = high


def make_kernel(n_row, n_col, coupling):
    def kernel(
        rec_hbm, face_ref, slot_ref, ps_ref, px_ref, x0_hbm,
        mig_out, inv_out,
        recs, pats, migs, opp, diag, own, xab, xba, pab, outs,
        hot, split, mig_l, mig_r, rpat, sel, mask, link,
        eaa, eab, eba, ebb,
        xaa_l, x1aa_l, xab_l, xba_l, xbb_l,
        xaa_r, xab_r, xba_r, xbb_r, paa_r, pab_r, pba_r, pbb_r,
        loc, rec_s, rec_r, pat_s, pat_r, mig_s, mig_rs, opp_s, opp_r, dia_s, dia_r, out_s,
    ):
        r = lax.axis_index("row")
        c = lax.axis_index("col")
        odd = r % 2
        s = 1 - 2 * odd
        west = (r, (c + n_col - 1) % n_col)
        east = (r, (c + 1) % n_col)
        near = ((r + s + n_row) % n_row, c)
        far = ((r - s + n_row) % n_row, c)
        ahead = ((r + 2 * s + n_row) % n_row, c)
        behind = ((r - 2 * s + n_row) % n_row, c)
        group = (3, 4, 2 - odd, 1 + odd)
        direct = ((west, EAST), (east, WEST), (near, NEAR))
        at_first, at_last = c % 8 == 0, c % 8 == 7
        is_relay = (c % 8 == 2) | (c % 8 == 5)
        back2, on2 = (r, (c + n_col - 2) % n_col), (r, (c + 2) % n_col)
        back3, on3 = (r, (c + n_col - 3) % n_col), (r, (c + 3) % n_col)
        detour = (
            ((r, jnp.where(at_first, on2[1], west[1])), jnp.where(at_first, RELAY, EAST)),
            ((r, jnp.where(at_last, back2[1], east[1])), jnp.where(at_last, RELAY, WEST)),
        )
        forth = c % 2 == 1
        goal = (r, jnp.where(forth, on3[1], back3[1]))
        goal_slot = jnp.where(forth, WEST, EAST)

        def cols(q):
            return pl.ds(pl.multiple_of(q * N, N), N)

        local = []

        def fetch(src, dst):
            copy = pltpu.make_async_copy(src, dst, loc.at[len(local)])
            copy.start()
            local.append(copy)

        fetch(rec_hbm, recs.at[4])
        fetch(x0_hbm.at[:, 0:N], own.at[X0])
        for slot in range(4):
            fetch(x0_hbm.at[:, cols(group[slot])], xab.at[slot])

        pats[4] = jnp.zeros((8, 128), F32)
        pats[4, 0:4, 0:20] = jnp.where(ps_ref[...] > 0, 1.0, 0.0).astype(F32)
        pats[4, 4:8, 0:20] = jnp.where(px_ref[...] > 0, 1.0, 0.0).astype(F32)

        barrier = pltpu.get_barrier_semaphore()
        for other in (west, east, near, far, ahead, behind, back2, on2, back3, on3):
            pl.semaphore_signal(barrier, inc=1, device_id=other, device_id_type=MESH)
        pl.semaphore_wait(barrier, 10)

        def send(src, dst, ssem, rsem, device):
            copy = pltpu.make_async_remote_copy(
                src_ref=src, dst_ref=dst, send_sem=ssem, recv_sem=rsem, device_id=device, device_id_type=MESH
            )
            copy.start()

        def arrive(dst, ssem, rsem):
            pltpu.make_async_remote_copy(
                src_ref=dst, dst_ref=dst, send_sem=ssem, recv_sem=rsem, device_id=near, device_id_type=MESH
            ).wait_recv()

        def sent(src, ssem):
            pltpu.make_async_remote_copy(
                src_ref=src, dst_ref=src, send_sem=ssem, recv_sem=loc.at[0], device_id=near, device_id_type=MESH
            ).wait_send()

        def rrows(j):
            return pl.ds(j * RROWS, RROWS)

        def crows(j):
            return pl.ds(pl.multiple_of(j * CROWS, CROWS), CROWS)

        relayed = []

        def relay(src, dst, ssem, here, there):
            copy = pltpu.make_async_remote_copy(
                src_ref=src, dst_ref=dst, send_sem=ssem, recv_sem=there, device_id=goal, device_id_type=MESH
            )
            relayed.append(copy)

            @pl.when(is_relay)
            def _():
                arrive(src, ssem, here)
                copy.start()

        for j in range(RCH):
            for way in (2, 0, 1):
                device, theirs = direct[way]
                send(rec_hbm.at[rrows(j)], recs.at[theirs, rrows(j)], rec_s.at[way, j], rec_r.at[theirs, j], device)
        for way in (2, 0, 1):
            device, theirs = direct[way]
            send(pats.at[4], pats.at[theirs], pat_s.at[way], pat_r.at[theirs], device)
        for slot, (device, theirs) in ((FAR, (far, FAR)), (NEAR, (near, NEAR)), (WEST, detour[0]), (EAST, detour[1])):
            send(x0_hbm.at[:, cols(group[slot])], opp.at[theirs], opp_s.at[slot], opp_r.at[theirs], device)

        place = face_ref[...] * N + slot_ref[...]
        place = jnp.transpose(jnp.broadcast_to(place.astype(F32), (N, N)))
        lane = lax.broadcasted_iota(jnp.int32, (N, N), 1).astype(F32)
        for slot in range(5):
            q = 0 if slot == 4 else group[slot]
            first = (q * N * jnp.ones((1, 1), jnp.int32)).astype(F32)
            hot[:, slot * N : (slot + 1) * N] = jnp.where(place == lane + first, 1.0, 0.0).astype(BF16)

        row8 = lax.broadcasted_iota(jnp.int32, (N, 8), 0) // BLK
        col8 = lax.broadcasted_iota(jnp.int32, (N, 8), 1)
        spread_s = jnp.where(col8 == row8, 1.0, 0.0).astype(BF16)
        spread_x = jnp.where(col8 == row8 + 4, 1.0, 0.0).astype(BF16)
        row128 = lax.broadcasted_iota(jnp.int32, (N, 128), 0) // BLK
        col128 = lax.broadcasted_iota(jnp.int32, (N, 128), 1)
        for slot in range(5):
            q = 0 if slot == 4 else group[slot]
            sel[slot] = jnp.where(col128 == row128 + q * 4, 1.0, 0.0).astype(BF16)
        mine = pats[4].astype(BF16)
        rpat[0] = dot(spread_s, mine).astype(BF16)
        rpat[1] = dot(spread_x, mine).astype(BF16)

        for j in range(RCH):
            sent(recs.at[4, rrows(j)], rec_s.at[2, j])
        for copy in local:
            copy.wait()

        for slot in range(5):
            mask[slot] = dot_nt(rpat[1], sel[slot])
            link[slot] = dot_nt(rpat[0], sel[slot]) * coupling
        for slot in range(4):
            mask[slot + 5] = dot_nt(sel[slot], rpat[1])
            link[slot + 5] = dot_nt(sel[slot], rpat[0]) * coupling
        for slot in range(4):
            block = xab[slot] * mask[slot]
            xab[slot] = block
            put_both(xab_l.at[slot], xab_r.at[slot], block)
        block = own[X0] * mask[4]
        own[X0] = block
        put_both(xaa_l, xaa_r, block)

        def three(slot):
            x = recs[slot]
            high = x.astype(BF16)
            rest = x - high.astype(F32)
            mid = rest.astype(BF16)
            low = (rest - mid.astype(F32)).astype(BF16)
            rows = pl.ds(pl.multiple_of(slot * N, N), N)
            split[rows, 0:FEAT] = high
            split[rows, FEAT : 2 * FEAT] = mid
            split[rows, 2 * FEAT : 3 * FEAT] = low

        three(4)

        for j in range(RCH):
            arrive(recs.at[NEAR, rrows(j)], rec_s.at[3, j], rec_r.at[NEAR, j])
            send(recs.at[NEAR, rrows(j)], recs.at[FAR, rrows(j)], rec_s.at[3, j], rec_r.at[FAR, j], ahead)
        arrive(pats.at[NEAR], pat_s.at[3], pat_r.at[NEAR])
        send(pats.at[NEAR], pats.at[FAR], pat_s.at[3], pat_r.at[FAR], ahead)
        three(NEAR)
        for slot in (WEST, EAST, FAR):
            for j in range(RCH):
                arrive(recs.at[slot, rrows(j)], rec_s.at[3, j], rec_r.at[slot, j])
            three(slot)
            arrive(pats.at[slot], pat_s.at[3], pat_r.at[slot])

        def spread(kind):
            for j in range(CH):
                for way in (2, 0, 1):
                    device, theirs = detour[way] if way < 2 and j in DETOUR[kind] else direct[way]
                    send(
                        own.at[kind, crows(j)], diag.at[kind, theirs, crows(j)],
                        dia_s.at[kind, way, j], dia_r.at[kind, theirs, j], device,
                    )

        def relay_diag(kind):
            for j in DETOUR[kind]:
                relay(
                    diag.at[kind, RELAY, crows(j)], diag.at[kind, goal_slot, crows(j)],
                    dia_s.at[kind, RELAY, j], dia_r.at[kind, RELAY, j], dia_r.at[kind, goal_slot, j],
                )

        def take(kind, slot):
            for j in range(CH):
                arrive(diag.at[kind, slot, crows(j)], dia_s.at[kind, 3, j], dia_r.at[kind, slot, j])

        def forward(kind, j):
            arrive(diag.at[kind, NEAR, crows(j)], dia_s.at[kind, 3, j], dia_r.at[kind, NEAR, j])
            send(
                diag.at[kind, NEAR, crows(j)], diag.at[kind, FAR, crows(j)],
                dia_s.at[kind, 3, j], dia_r.at[kind, FAR, j], ahead,
            )

        def forward_all(kind):
            for j in range(CH):
                forward(kind, j)

        parts = dot(hot[...], split[...])
        migrated = (parts[:, 0:FEAT] + parts[:, FEAT : 2 * FEAT]) + parts[:, 2 * FEAT : 3 * FEAT]
        migs[4] = migrated
        for j in range(RCH):
            for way in (2, 0, 1):
                device, theirs = direct[way]
                send(migs.at[4, rrows(j)], migs.at[theirs, rrows(j)], mig_s.at[way, j], mig_rs.at[theirs, j], device)
        mig_copy = pltpu.make_async_copy(migs.at[4], mig_out, out_s.at[5])
        mig_copy.start()

        def put_mig(slot):
            high, low = halves(migs[slot])
            mig_l[slot, :, 0:FEAT] = high
            mig_l[slot, :, FEAT : 2 * FEAT] = high
            mig_l[slot, :, 2 * FEAT : 3 * FEAT] = low
            mig_r[slot, :, 0:FEAT] = high
            mig_r[slot, :, FEAT : 2 * FEAT] = low
            mig_r[slot, :, 2 * FEAT : 3 * FEAT] = high

        relay(opp.at[RELAY], opp.at[goal_slot], opp_s.at[RELAY], opp_r.at[RELAY], opp_r.at[goal_slot])

        for slot in range(4):
            link[slot + 9] = dot_nt(dot(spread_s, pats[slot].astype(BF16)).astype(BF16), sel[4]) * coupling
        put_mig(4)
        put_left(eaa, dot_nt(mig_l[4], mig_r[4]) * link[4])
        own[P1] = own[X0] + dot(eaa[...], xaa_r[...])
        for slot in range(4):
            pab[slot] = xab[slot] + dot(eaa[...], xab_r[slot])

        for j in range(RCH):
            arrive(migs.at[NEAR, rrows(j)], mig_s.at[3, j], mig_rs.at[NEAR, j])
            send(migs.at[NEAR, rrows(j)], migs.at[FAR, rrows(j)], mig_s.at[3, j], mig_rs.at[FAR, j], ahead)
        spread(X0)

        def couple(*slots):
            for slot in slots:
                put_mig(slot)
            for slot in slots:
                put_left(eab.at[slot], dot_nt(mig_l[4], mig_r[slot]) * link[slot])

        def couple_back(*slots):
            for slot in slots:
                put_left(eba.at[slot], dot_nt(mig_l[slot], mig_r[4]) * link[slot + 5])
                put_left(ebb.at[slot], dot_nt(mig_l[slot], mig_r[slot]) * link[slot + 9])

        def arrive_mig(slot):
            for j in range(RCH):
                arrive(migs.at[slot, rrows(j)], mig_s.at[3, j], mig_rs.at[slot, j])

        def take_opp(*slots):
            for slot in slots:
                arrive(opp.at[slot], opp_s.at[slot], opp_r.at[slot])
            for slot in slots:
                block = opp[slot] * mask[slot + 5]
                xba[slot] = block
                put_both(xba_l.at[slot], xba_r.at[slot], block)

        def back_product(*slots):
            for slot in slots:
                block = xba[slot] + dot(ebb[slot], xba_r[slot]) + dot(eba[slot], xaa_r[...])
                put_right(pba_r.at[slot], block * mask[slot + 5])

        arrive_mig(WEST)
        arrive_mig(EAST)
        couple(WEST, EAST, NEAR)
        take_opp(WEST, EAST, NEAR, FAR)
        own[P1] = own[P1] + dot(eab[WEST], xba_r[WEST]) + dot(eab[EAST], xba_r[EAST]) + dot(eab[NEAR], xba_r[NEAR])
        couple_back(WEST, EAST)
        back_product(WEST, EAST)
        own[X1] = 2.0 * own[X0] - dot(xab_l[WEST], pba_r[WEST]) - dot(xab_l[EAST], pba_r[EAST])

        relay_diag(X0)
        arrive_mig(FAR)
        couple(FAR)
        block = (own[P1] + dot(eab[FAR], xba_r[FAR])) * mask[4]
        own[P1] = block
        spread(P1)
        put_right(paa_r, block)
        couple_back(NEAR, FAR)
        back_product(NEAR, FAR)
        block = own[X1] - dot(xab_l[NEAR], pba_r[NEAR]) - dot(xab_l[FAR], pba_r[FAR]) - dot(xaa_l[...], paa_r[...])
        block = block * mask[4]
        own[X1] = block
        spread(X1)
        put_both(x1aa_l, xaa_r, block)
        forward_all(X0)

        def next_back(*slots):
            for slot in slots:
                put_both(xbb_l.at[slot], xbb_r.at[slot], diag[X0, slot])
            for slot in slots:
                block = 2.0 * xba[slot] - dot(xbb_l[slot], pba_r[slot]) - dot(xba_l[slot], paa_r[...])
                block = block * mask[slot + 5]
                xba[slot] = block
                put_right(xba_r.at[slot], block)

        take(X0, WEST)
        take(X0, EAST)
        next_back(WEST, EAST, NEAR)
        own[P2] = (
            own[X1] + dot(eaa[...], xaa_r[...])
            + dot(eab[WEST], xba_r[WEST]) + dot(eab[EAST], xba_r[EAST]) + dot(eab[NEAR], xba_r[NEAR])
        )
        relay_diag(P1)
        take(X0, FAR)
        next_back(FAR)
        block = (own[P2] + dot(eab[FAR], xba_r[FAR])) * mask[4]
        own[P2] = block
        spread(P2)
        put_right(paa_r, block)

        def ahead_product(*slots):
            for slot in slots:
                block = pab[slot] + dot(eab[slot], xbb_r[slot])
                put_right(pab_r.at[slot], block * mask[slot])
            for slot in slots:
                xab[slot] = 2.0 * xab[slot] - dot(xaa_l[...], pab_r[slot])

        forward_all(P1)
        ahead_product(WEST, EAST, NEAR, FAR)
        back_product(WEST, EAST, NEAR, FAR)
        outs[4] = 2.0 * own[X1] - dot(x1aa_l[...], paa_r[...])
        forward_all(X1)
        relay_diag(X1)

        def first_ahead(*slots):
            for slot in slots:
                put_right(pbb_r.at[slot], diag[P1, slot])
            for slot in slots:
                block = (xab[slot] - dot(xab_l[slot], pbb_r[slot])) * mask[slot]
                xab[slot] = block
                put_both(xab_l.at[slot], xab_r.at[slot], block)

        take(P1, WEST)
        take(P1, EAST)
        first_ahead(WEST, EAST, NEAR)
        take(P1, FAR)
        first_ahead(FAR)
        block = outs[4] - dot(xab_l[WEST], pba_r[WEST]) - dot(xab_l[EAST], pba_r[EAST])
        outs[4] = (block - dot(xab_l[NEAR], pba_r[NEAR]) - dot(xab_l[FAR], pba_r[FAR])) * mask[4]
        out_copies = [pltpu.make_async_copy(outs.at[4], inv_out.at[:, 0:N], out_s.at[4])]
        out_copies[0].start()

        def second_product(*slots):
            for slot in slots:
                put_right(xbb_r.at[slot], diag[X1, slot])
            for slot in slots:
                block = xab[slot] + dot(eaa[...], xab_r[slot]) + dot(eab[slot], xbb_r[slot])
                put_right(pab_r.at[slot], block * mask[slot])
            for slot in slots:
                xab[slot] = 2.0 * xab[slot] - dot(x1aa_l[...], pab_r[slot])

        take(X1, WEST)
        take(X1, EAST)
        second_product(WEST, EAST, NEAR)
        forward_all(P2)
        relay_diag(P2)
        take(X1, FAR)
        second_product(FAR)

        def finish(*slots):
            for slot in slots:
                put_right(pbb_r.at[slot], diag[P2, slot])
            for slot in slots:
                outs[slot] = (xab[slot] - dot(xab_l[slot], pbb_r[slot])) * mask[slot]
            for slot in slots:
                copy = pltpu.make_async_copy(outs.at[slot], inv_out.at[:, cols(group[slot])], out_s.at[slot])
                copy.start()
                out_copies.append(copy)

        take(P2, WEST)
        take(P2, EAST)
        finish(WEST, EAST, NEAR)
        take(P2, FAR)
        finish(FAR)

        def sent_diag(way):
            def sent_kind(kind, carry):
                for j in range(CH):
                    sent(own.at[kind, crows(j)], dia_s.at[kind, way, j])
                return carry

            lax.fori_loop(0, 4, sent_kind, 0)

        def sent_way(way, carry):
            sent(pats.at[4], pat_s.at[way])
            sent(opp.at[way], opp_s.at[way])
            for j in range(RCH):
                sent(migs.at[4, rrows(j)], mig_s.at[way, j])
            return carry

        lax.fori_loop(0, 4, sent_way, 0)
        for way in (0, 1, 3):
            for j in range(RCH):
                sent(recs.at[4, rrows(j)], rec_s.at[way, j])
        for way in range(4):
            sent_diag(way)

        @pl.when(is_relay)
        def _():
            for copy in relayed:
                copy.wait_send()

        mig_copy.wait()
        for copy in out_copies:
            copy.wait()

    return kernel


def hand_over(mig_in, inv_in, mig_out, inv_out):
    mig_out[...] = mig_in[...]
    inv_out[...] = inv_in[...]


def solution(mesh):
    n_row, n_col = mesh.shape["row"], mesh.shape["col"]
    coupling = COUPLE_BASE / math.sqrt(5 * FEAT * N)
    vmem = pl.BlockSpec(memory_space=pltpu.VMEM)
    hbm = pl.BlockSpec(memory_space=pl.ANY)
    dma = pltpu.SemaphoreType.DMA

    def f32(*shape):
        return pltpu.VMEM(shape, F32)

    def bf16(*shape):
        return pltpu.VMEM(shape, BF16)

    left = bf16(N, 3 * N)
    left4 = bf16(4, N, 3 * N)
    right = bf16(3 * N, N)
    right4 = bf16(4, 3 * N, N)

    def body(records, move_face, move_slot, pattern_s, pattern_x, start_inverse):
        shapes = (jax.ShapeDtypeStruct((N, FEAT), F32), jax.ShapeDtypeStruct((N, 5 * N), F32))
        results = pl.pallas_call(
            make_kernel(n_row, n_col, coupling),
            out_shape=shapes,
            in_specs=[hbm, vmem, vmem, vmem, vmem, hbm],
            out_specs=(hbm, hbm),
            scratch_shapes=[
                f32(5, N, FEAT), f32(5, 8, 128), f32(5, N, FEAT), f32(5, N, N), f32(4, 5, N, N), f32(4, N, N),
                f32(4, N, N), f32(4, N, N), f32(4, N, N), f32(5, N, N),
                bf16(N, 5 * N), bf16(5 * N, 3 * FEAT), bf16(5, N, 3 * FEAT), bf16(5, N, 3 * FEAT),
                bf16(2, N, 128), bf16(5, N, 128), f32(9, N, N), f32(13, N, N),
                left, left4, left4, left4,
                left, left, left4, left4, left4,
                right, right4, right4, right4, right, right4, right4, right4,
                dma((6,)), dma((4, RCH)), dma((4, RCH)), dma((4,)), dma((4,)), dma((4, RCH)), dma((4, RCH)),
                dma((5,)), dma((5,)), dma((4, 5, CH)), dma((4, 5, CH)), dma((6,)),
            ],
            compiler_params=pltpu.CompilerParams(
                collective_id=0, has_side_effects=True, vmem_limit_bytes=56 << 20
            ),
            cost_estimate=pl.CostEstimate(flops=8 * 10**9, bytes_accessed=3 * 2**20, transcendentals=0),
            name="hotelling",
        )(
            records,
            move_face.reshape(1, N),
            move_slot.reshape(1, N),
            pattern_s,
            pattern_x,
            start_inverse,
        )
        return pl.pallas_call(
            hand_over,
            out_shape=shapes,
            in_specs=[vmem, vmem],
            out_specs=(vmem, vmem),
            name="hand_over",
        )(*results)

    split = P(("row", "col"))
    wide = P(("row", "col"), None)
    return jax.shard_map(
        body,
        mesh=mesh,
        in_specs=(wide, split, split, wide, wide, wide),
        out_specs=(wide, wide),
        check_vma=False,
    )
```
